128 devices in a mesh: tok: 16 (over y, x), exp: 8 (over z, core).
Axes of the slice: x: 4, y: 4, z: 4, core: 2. Of those that a mesh axis runs over, the one named last changes fastest.
Arguments:
- tokens: bfloat16 [16384, 2560], P('exp', 'tok'), may hold values from -6 to 6
- grad_out: bfloat16 [16384, 2560], P('exp', 'tok'), may hold values from -6 to 6
- gate_probs: float32 [16384, 6], P('exp'), may hold values from 0.05 to 0.5
- routes: int32 [16384, 6], P('exp'), may hold values from 0 to 15, all different within a row; in each aligned block of 2048 rows (0 to 2047, 2048 to 4095, ...) at most 1536 rows name the same one
- need_lists: int32 [8, 16], replicated, may hold values from 0 to 79, as said below
- up_weight: bfloat16 [80, 2560, 768], P('exp', 'tok'), may hold values from -0.125 to 0.125
- down_weight: bfloat16 [80, 2560, 768], P('exp', 'tok'), may hold values from -0.21875 to 0.21875
Outputs:
- token_grads: bfloat16 [16384, 2560], P('exp', 'tok')
- gate_grads: float32 [16384, 6], P('exp')
- up_grads: bfloat16 [80, 2560, 768], P('exp', 'tok')
- down_grads: bfloat16 [80, 2560, 768], P('exp', 'tok')
The draws below stay inside these ranges and needn't reach their ends.
Inputs may be any that keep to these rules, and one draw needn't show every extreme that they name: `routes`: within each aligned block of 2048 rows (one index of exp) a row names 6 different slots; no slot is named by more than 1536 rows of a block, and in every draw some slot is named by exactly 1536 rows of some block. `need_lists`: each row holds 16 different experts; entries 2 * o to 2 * o + 1 of a row lie in o * 10 to o * 10 + 9, the experts of exp index o.
All inputs are finite; a program needn't handle non-finite values.
Results may differ from the reference program's by a relative error of at most 0.007.
Values may be sent and summed in bfloat16 or wider, within the bound.
A program may use at most 384 MiB of HBM per device.

```python
import math
import jax
import jax.numpy as jnp
import numpy as np
from jax import lax

D = 2560
H = 768
E = 80
TOPK = 6
R_COL = 2048
EXP_DEV = 10
PER_OWN = 2
CAP = 1536
TOKENS = 16384
N_TOK = 16
N_EXP = 8


def draw_need_lists(key, part):
    key = jax.random.fold_in(key, 11)

    def pick_entries(flat_id):
        column_id = flat_id // N_EXP
        owner_id = flat_id % N_EXP
        shuffled = jax.random.permutation(jax.random.fold_in(key, flat_id), EXP_DEV)
        leading = jnp.where(column_id == 0, EXP_DEV - 1, jnp.where(column_id == 1, 0, shuffled[0]))
        shuffled = (shuffled - shuffled[0] + leading) % EXP_DEV
        return owner_id * EXP_DEV + shuffled[:PER_OWN]
    picked = jax.vmap(pick_entries)(jnp.arange(N_EXP * N_EXP, dtype=jnp.int32))
    return picked.reshape(N_EXP, N_EXP * PER_OWN).astype(jnp.int32)


def block_scale(rng, dims, split, smallest, largest):
    level, own = 1.0, jax.random.fold_in(rng, 6)
    for axis_at, parts in split:
        draws = jnp.exp(jax.random.uniform(jax.random.fold_in(own, axis_at), (parts,), jnp.float32, smallest / len(split), largest / len(split)))
        level = level * jnp.repeat(draws, dims[axis_at] // parts).reshape([-1 if axis == axis_at else 1 for axis in range(len(dims))])
    return level


def assign_block(stream_key, own, number, rows, count, top, limit, lean):
    order = jax.random.permutation(stream_key, count)
    crowded, common = load_shares(count, rows * top, limit, lean, True), load_shares(count, rows * top, limit, lean, False)
    places = jnp.arange(count)

    def named(tallies, rotation):
        used = int((tallies > 0).sum())
        fixed = max(1, used // 4)
        moved = fixed + (places - fixed + rotation * (used - fixed)) % max(1, count - fixed)
        return jnp.zeros((count,), jnp.int32).at[order[jnp.where(places < fixed, places, moved)]].set(jnp.asarray(tallies, jnp.int32))

    tallies = jnp.where(number % 4 == 0, named(crowded, number // 4), named(common, number - number // 4 - 1))
    mixed = jax.random.permutation(jax.random.fold_in(own, 3), count)
    source_of, taker = mixed[0:count // 2 * 2:2], mixed[1:count // 2 * 2:2]
    room = jnp.minimum(tallies[source_of] - 1, limit - tallies[taker]) // 2
    room = jnp.where((source_of == order[0]) | (taker == order[0]) | (tallies[taker] == 0), 0, jnp.maximum(room, 0))
    moved = jax.random.randint(jax.random.fold_in(own, 4), (count // 2,), 0, 1 << 20) % (room + 1)
    tallies = tallies.at[source_of].add(-moved).at[taker].add(moved)
    items = jnp.searchsorted(jnp.cumsum(tallies), jnp.arange(rows * top), side="right").astype(jnp.int32)
    grid = items.reshape(top, rows).T
    grid = grid[jax.random.permutation(jax.random.fold_in(own, 1), rows)]
    rotation = jax.random.randint(jax.random.fold_in(own, 2), (rows, 1), 0, top)
    return jnp.take_along_axis(grid, (jnp.arange(top)[None, :] + rotation) % top, axis=1)


def load_shares(amount, total, limit, lean, full):
    portions = [(1 << 20) // math.isqrt(grade ** lean) + 1 for grade in range(1, amount + 1)]
    largest = limit if full else min(limit, max(-(-total // amount), total * portions[0] // sum(portions)))
    least = 1 if total - largest >= amount - 1 else 0
    given, spare = [largest] + [least] * (amount - 1), total - largest - least * (amount - 1)
    while spare > 0:
        movable = [i for i in range(1, amount) if given[i] < largest] or [i for i in range(1, amount) if given[i] < limit]
        mass, budget = sum([portions[i] for i in movable]), spare
        for i in movable:
            addition = min(limit - given[i], max(1, budget * portions[i] // mass), spare)
            given[i] = given[i] + addition
            spare = spare - addition
    return np.array(given)


def centred(key, shape, deviation, reach, split=(), held_as=jnp.bfloat16):
    entries = deviation * jax.random.normal(key, shape, jnp.float32)
    if split:
        entries = entries * block_scale(key, shape, split, -0.22, 0.18)
    return jnp.clip(entries, -reach, reach).astype(held_as)


def setup_inputs(seed: int = 0) -> dict:
    key_list = jax.random.split(jax.random.key(seed), 8)
    tokens = centred(key_list[0], (TOKENS, D), 1.0, 6.0, ((0, 8), (1, 16)))
    grad_out = centred(key_list[1], (TOKENS, D), 1.0, 6.0, ((0, 8), (1, 16)))
    gate_probs = jnp.clip(0.05 + 0.45 * jax.random.uniform(key_list[2], (TOKENS, TOPK), jnp.float32) ** block_scale(key_list[2], (TOKENS, TOPK), ((0, 8),), -0.2, 0.2), 0.05, 0.5)
    routes_keys = jax.random.split(jax.random.fold_in(key_list[3], 1), TOKENS // R_COL)
    routes_turns = jax.random.permutation(jax.random.fold_in(key_list[3], 3), TOKENS // R_COL)
    routes = jax.vmap(lambda own, number: assign_block(jax.random.fold_in(key_list[3], 2), own, number, R_COL, N_TOK, TOPK, CAP, 1))(routes_keys, routes_turns).reshape((TOKENS, TOPK))
    need_lists = draw_need_lists(jax.random.fold_in(key_list[7], 71), 0)
    up_weight = centred(key_list[5], (E, D, H), D ** -0.5, 0.125, ((0, 8), (1, 16)))
    down_weight = centred(key_list[6], (E, D, H), H ** -0.5, 0.21875, ((0, 8), (1, 16)))
    return {"tokens": tokens, "grad_out": grad_out, "gate_probs": gate_probs, "routes": routes, "need_lists": need_lists, "up_weight": up_weight, "down_weight": down_weight}


def silu_parts(pre_act):
    sigmoid_value = jax.nn.sigmoid(pre_act)
    return pre_act * sigmoid_value, sigmoid_value * (1.0 + pre_act * (1.0 - sigmoid_value))


def reference(tokens, grad_out, gate_probs, routes, need_lists, up_weight, down_weight):
    row_ids = jnp.arange(R_COL, dtype=jnp.int32)
    cap_ids = jnp.arange(CAP, dtype=jnp.int32)

    def add_pair(totals, flat_id):
        token_acc, prob_acc, up_acc, down_acc = totals
        column = (flat_id // N_TOK).astype(jnp.int32)
        slot_id = (flat_id % N_TOK).astype(jnp.int32)
        row_start = (column * R_COL).astype(jnp.int32)
        token_col = lax.dynamic_slice_in_dim(tokens, row_start, R_COL, 0)
        grad_col = lax.dynamic_slice_in_dim(grad_out, row_start, R_COL, 0)
        prob_col = lax.dynamic_slice_in_dim(gate_probs, row_start, R_COL, 0)
        route_col = lax.dynamic_slice_in_dim(routes, row_start, R_COL, 0)
        slot_hits = route_col == slot_id
        member = jnp.any(slot_hits, axis=1)
        prob_rows = jnp.sum(jnp.where(slot_hits, prob_col, 0.0), axis=1)
        position = (jnp.cumsum(member.astype(jnp.int32)) - 1).astype(jnp.int32)
        matched = (position[None, :] == cap_ids[:, None]) & member[None, :]
        indices = jnp.sum(jnp.where(matched, row_ids[None, :], 0), axis=1).astype(jnp.int32)
        filled = jnp.any(matched, axis=1)
        slot_prob = jnp.where(filled, prob_rows[indices], 0.0)
        expert = need_lists[column, slot_id].astype(jnp.int32)
        up_matrix = lax.dynamic_index_in_dim(up_weight, expert, 0, keepdims=False)
        down_matrix = lax.dynamic_index_in_dim(down_weight, expert, 0, keepdims=False)
        token_rows = token_col[indices] * filled[:, None].astype(token_col.dtype)
        grad_rows = grad_col[indices] * filled[:, None].astype(grad_col.dtype)
        pre_act = jnp.dot(token_rows, up_matrix, preferred_element_type=jnp.float32)
        activated, silu_slope = silu_parts(pre_act)
        activation = activated.astype(jnp.bfloat16)
        hidden_grad = jnp.dot(grad_rows, down_matrix, preferred_element_type=jnp.float32)
        prob_grad = jnp.sum(activation.astype(jnp.float32) * hidden_grad, axis=1)
        pre_grad = (slot_prob[:, None] * hidden_grad * silu_slope).astype(jnp.bfloat16)
        scaled = (slot_prob[:, None] * grad_rows.astype(jnp.float32)).astype(jnp.bfloat16)
        input_part = lax.dot_general(pre_grad, up_matrix, (((1,), (1,)), ((), ())), preferred_element_type=jnp.float32)
        input_part = jnp.where(filled[:, None], input_part, 0.0)
        grad_up = lax.dot_general(token_rows, pre_grad, (((0,), (0,)), ((), ())), preferred_element_type=jnp.float32).astype(jnp.bfloat16)
        grad_down = lax.dot_general(scaled, activation, (((0,), (0,)), ((), ())), preferred_element_type=jnp.float32).astype(jnp.bfloat16)
        token_acc = token_acc.at[row_start + indices].add(input_part)
        token_grad = jnp.zeros((R_COL,), jnp.float32).at[indices].add(jnp.where(filled, prob_grad, 0.0))
        prob_block = lax.dynamic_slice_in_dim(prob_acc, row_start, R_COL, 0)
        prob_block = prob_block + jnp.where(slot_hits, token_grad[:, None], 0.0)
        prob_acc = lax.dynamic_update_slice_in_dim(prob_acc, prob_block, row_start, 0)
        up_acc = up_acc.at[expert].add(grad_up.astype(jnp.float32))
        down_acc = down_acc.at[expert].add(grad_down.astype(jnp.float32))
        return (token_acc, prob_acc, up_acc, down_acc), None

    initial = (jnp.zeros(tokens.shape, jnp.float32), jnp.zeros(gate_probs.shape, jnp.float32),
               jnp.zeros(up_weight.shape, jnp.float32), jnp.zeros(down_weight.shape, jnp.float32))
    totals, unused = lax.scan(add_pair, initial, jnp.arange(N_EXP * N_TOK, dtype=jnp.int32))
    return (totals[0].astype(jnp.bfloat16), totals[1], totals[2].astype(jnp.bfloat16), totals[3].astype(jnp.bfloat16))
```

```python
import functools

import jax
import jax.numpy as jnp
from jax import lax
from jax.experimental import pallas as pl
from jax.experimental.pallas import tpu as pltpu
from jax.sharding import PartitionSpec as P

MESH = pl.DeviceIdType.MESH
F32 = jnp.float32
BF16 = jnp.bfloat16


def loop(count, step):
    def run(i, carry):
        step(i)
        return carry

    lax.fori_loop(0, count, run, 0)


def layer_kernel(
    nt, ne, rows_dev, hid, cols, htile, ntile,
    sw, xs, p2,
    relay1, relay2, wout, trecv, gpart,
    xg, ww, pa, dw, cbuf, wt, pr, grow,
    s1, r1, st, tr, s2, wr, sf, ps, prs, sd, r2, sg, gr, cs, cr, ts, trr, fs, fr,
):
    t = lax.axis_index("tok")
    e = lax.axis_index("exp")
    z, k = lax.div(e, 2), lax.rem(e, 2)
    q, h = lax.div(t, 2), lax.rem(t, 2)
    nz = ne // 2
    sibling = 2 * z + 1 - k
    column_core = 2 * z + h

    def remote(src, dst, send, recv, tok, ex):
        return pltpu.make_async_remote_copy(
            src_ref=src, dst_ref=dst, send_sem=send, recv_sem=recv,
            device_id=(tok, ex), device_id_type=MESH,
        )

    def push(src, dst, send, recv, tok, ex):
        own = jnp.logical_and(tok == t, ex == e)

        @pl.when(own)
        def _():
            pltpu.make_async_copy(src, dst, recv).start()

        @pl.when(jnp.logical_not(own))
        def _():
            remote(src, dst, send, recv, tok, ex).start()

    def sent(src, dst, send, recv, tok, ex):
        @pl.when(jnp.logical_not(jnp.logical_and(tok == t, ex == e)))
        def _():
            remote(src, dst, send, recv, tok, ex).wait_send()

    def landed(dst, recv):
        pltpu.make_async_copy(dst, dst, recv).wait()

    def rows(block, count=1):
        size = rows_dev * count
        return pl.ds(pl.multiple_of(block * size, size), size)

    barrier = pltpu.get_barrier_semaphore()

    def greet_plane(i):
        tok, ex = lax.div(i, 2), 2 * z + lax.rem(i, 2)

        @pl.when(jnp.logical_not(jnp.logical_and(tok == t, ex == e)))
        def _():
            pl.semaphore_signal(barrier, inc=1, device_id=(tok, ex), device_id_type=MESH)

    def greet_line(ex):
        @pl.when(lax.div(ex, 2) != z)
        def _():
            pl.semaphore_signal(barrier, inc=1, device_id=(t, ex), device_id_type=MESH)

    loop(2 * nt, greet_plane)
    loop(ne, greet_line)
    pl.semaphore_wait(barrier, 2 * nt - 1 + ne - 2)

    def line_copy(i):
        dz, half, core = lax.div(i, 4), lax.rem(lax.div(i, 2), 2), lax.rem(i, 2)
        plane = lax.rem(z + dz, nz)
        piece = (2 * plane + half) * 2 + core
        m = half * ne + e
        return (sw.at[piece], relay1.at[m], s1.at[i], r1.at[m], t, 2 * plane + core)

    def token_copy(i):
        place = lax.rem(q + i, ne)
        return (xs, xg.at[:, rows(t), :], st.at[i], tr.at[t], 2 * place + k, 2 * z + lax.rem(q, 2))

    def plane_copy(i):
        tok = lax.rem(t + i, nt)
        m = lax.rem(tok, 2) * ne + lax.div(tok, 2)
        return (relay1.at[m], ww.at[:, rows(t), :], s2.at[i], wr.at[t], tok, e)

    def twin_copy(i):
        block = 4 * lax.div(i, 2) + 2 * k + lax.rem(i, 2)
        part = xg.at[:, rows(block), :]
        return (part, part, sf.at[i], tr.at[block], t, sibling)

    prob_copy = remote(p2.at[1 - k], pr, ps, prs, t, sibling)
    prob_copy.start()
    loop(ne, lambda i: push(*token_copy(i)))
    loop(2 * ne, lambda i: push(*line_copy(i)))

    def forward_weights(i):
        src, dst, send, recv, tok, ex = plane_copy(i)
        m = lax.rem(tok, 2) * ne + lax.div(tok, 2)
        landed(src, r1.at[m])
        push(src, dst, send, recv, tok, ex)

    loop(nt, forward_weights)

    def forward_tokens(i):
        block = 4 * lax.div(i, 2) + 2 * k + lax.rem(i, 2)
        landed(xg.at[:, rows(block), :], tr.at[block])
        remote(*twin_copy(i)).start()

    loop(nt // 2, forward_tokens)

    def take_tokens(i):
        block = 4 * lax.div(i, 2) + 2 * (1 - k) + lax.rem(i, 2)
        landed(xg.at[:, rows(block), :], tr.at[block])

    loop(nt // 2, take_tokens)
    loop(nt, lambda i: landed(ww.at[:, rows(i), :], wr.at[i]))
    prob_copy.wait()
    loop(ne, lambda i: sent(*token_copy(i)))
    loop(2 * ne, lambda i: sent(*line_copy(i)))
    loop(nt, lambda i: sent(*plane_copy(i)))
    loop(nt // 2, lambda i: remote(*twin_copy(i)).wait_send())

    grow[...] = jnp.zeros_like(grow)
    mine = jnp.where(k == h, 1.0, 0.0).astype(F32)

    def hidden(hi):
        units = pl.ds(pl.multiple_of(hi * htile, htile), htile)
        wt[0] = ww[0, :, units].T
        wt[1] = ww[1, :, units].T

        def strip(ni):
            lanes = pl.ds(pl.multiple_of(ni * ntile, ntile), ntile)
            pre = jnp.dot(wt[0], xg[0, :, lanes], preferred_element_type=F32)
            hg = jnp.dot(wt[1], xg[1, :, lanes], preferred_element_type=F32)
            prob = p2[k, :, lanes] * mine + pr[:, lanes] * (1.0 - mine)
            sig = 1.0 / (1.0 + jnp.exp(-pre))
            act = (pre * sig).astype(BF16).astype(F32)
            slope = sig * (1.0 + pre * (1.0 - sig))
            pa[0, units, lanes] = (prob * hg * slope).astype(BF16)
            pa[1, units, lanes] = (prob * act).astype(BF16)
            grow[:, lanes] = grow[:, lanes] + jnp.sum(act * hg, axis=0, keepdims=True)

        loop(cols // ntile, strip)

    loop(hid // htile, hidden)

    def gate_copy(i):
        j = 2 * q + k
        return (grow, gpart.at[j], sg.at[i], gr.at[j], lax.rem(t + i, nt), column_core)

    loop(nt, lambda i: push(*gate_copy(i)))

    def grad_copy(block):
        m = h * ne + q
        return (dw.at[:, rows(block), :], relay2.at[m], sd.at[block], r2.at[m], block, e)

    def weight_grads(s):
        pair = lax.rem(q + s, ne)
        for a in range(2):
            dw[a, rows(pair, 2), :] = lax.dot_general(
                xg[a, rows(pair, 2), :], pa[a], (((1,), (1,)), ((), ())), preferred_element_type=F32
            ).astype(BF16)
        for w in range(2):
            push(*grad_copy(2 * pair + w))

    loop(ne, weight_grads)

    def pair_copy(u):
        pair = 2 * u + 1 - k
        return (xg.at[0, rows(pair, 2), :], cbuf.at[u], cs.at[u], cr.at[u], t, sibling)

    def block_copy(u, w):
        block = 2 * (2 * u + k) + w
        return (xg.at[0, rows(block), :], trecv.at[q], ts.at[2 * u + w], trr.at[q], block, column_core)

    def strips(pair, add):
        def strip(ni):
            lanes = pl.ds(pl.multiple_of(ni * ntile, ntile), ntile)
            part = jnp.dot(ww[0, rows(pair, 2), :], pa[0, :, lanes], preferred_element_type=F32)
            if add is not None:
                part = part + cbuf[add, :, lanes].astype(F32)
            xg[0, rows(pair, 2), lanes] = part.astype(BF16)

        loop(cols // ntile, strip)

    def give(u):
        strips(2 * u + 1 - k, None)
        remote(*pair_copy(u)).start()

    def keep(u):
        landed(cbuf.at[u], cr.at[u])
        strips(2 * u + k, u)
        for w in range(2):
            push(*block_copy(u, w))

    loop(ne // 2, give)
    loop(ne // 2, keep)

    def owner_copy(i):
        place, half = lax.rem(q + ne - lax.div(i, 2), ne), lax.rem(i, 2)
        piece = (2 * z + half) * 2 + k
        return (relay2.at[half * ne + place], wout.at[piece], fs.at[i], fr.at[piece], t, place)

    def forward_grads(i):
        place, half = lax.rem(q + ne - lax.div(i, 2), ne), lax.rem(i, 2)
        m = half * ne + place
        landed(relay2.at[m], r2.at[m])
        push(*owner_copy(i))

    loop(2 * ne, forward_grads)

    loop(2 * ne, lambda i: landed(wout.at[i], fr.at[i]))
    loop(ne, lambda i: landed(trecv.at[i], trr.at[i]))
    loop(nt, lambda i: landed(gpart.at[i], gr.at[i]))
    loop(nt, lambda i: sent(*gate_copy(i)))
    loop(nt, lambda i: sent(*grad_copy(i)))
    loop(ne // 2, lambda u: remote(*pair_copy(u)).wait_send())
    for w in range(2):
        loop(ne // 2, lambda u: sent(*block_copy(u, w)))
    loop(2 * ne, lambda i: sent(*owner_copy(i)))


def layer(sw, xs, p2, nt, ne):
    pieces, _, rows_dev, hid = sw.shape
    cols = xs.shape[2]
    width = nt * rows_dev
    htile, ntile = min(256, hid), min(512, cols)
    dma = pltpu.SemaphoreType.DMA
    anywhere = pl.BlockSpec(memory_space=pl.ANY)
    counts = (2 * ne, 2 * ne, ne, nt, nt, nt, nt // 2)
    counts_back = (nt, 2 * ne, nt, nt, ne // 2, ne // 2, ne, ne, 2 * ne, 2 * ne)
    return pl.pallas_call(
        functools.partial(layer_kernel, nt, ne, rows_dev, hid, cols, htile, ntile),
        out_shape=(
            jax.ShapeDtypeStruct(sw.shape, BF16),
            jax.ShapeDtypeStruct(sw.shape, BF16),
            jax.ShapeDtypeStruct(sw.shape, BF16),
            jax.ShapeDtypeStruct((ne, rows_dev, cols), BF16),
            jax.ShapeDtypeStruct((nt, 1, cols), F32),
        ),
        in_specs=[anywhere, anywhere, pl.BlockSpec(memory_space=pltpu.VMEM)],
        out_specs=(anywhere,) * 5,
        scratch_shapes=[
            pltpu.VMEM((2, width, cols), BF16),
            pltpu.VMEM((2, width, hid), BF16),
            pltpu.VMEM((2, hid, cols), BF16),
            pltpu.VMEM((2, width, hid), BF16),
            pltpu.VMEM((ne // 2, 2 * rows_dev, cols), BF16),
            pltpu.VMEM((2, htile, width), BF16),
            pltpu.VMEM((1, cols), F32),
            pltpu.VMEM((1, cols), F32),
            *[dma((count,)) for count in counts],
            dma,
            dma,
            *[dma((count,)) for count in counts_back],
        ],
        compiler_params=pltpu.CompilerParams(
            collective_id=0, has_side_effects=True, vmem_limit_bytes=60 * 1024 * 1024
        ),
        cost_estimate=pl.CostEstimate(
            flops=10 * width * hid * cols, bytes_accessed=64 << 20, transcendentals=hid * cols
        ),
    )(sw, xs, p2)


def combine_kernel(ids, pieces, up_out, down_out, total):
    total[...] = jnp.zeros_like(total)
    for n in range(pieces.shape[0]):
        expert = ids[n]
        for a in range(2):
            total[a, expert] = total[a, expert] + pieces[n, a].astype(F32)
    up_out[...] = total[0].astype(BF16)
    down_out[...] = total[1].astype(BF16)


def combine(ids, pieces, experts):
    count, _, rows_dev, hid = pieces.shape
    tile = 32 if rows_dev % 32 == 0 else 16
    out = jax.ShapeDtypeStruct((experts, rows_dev, hid), BF16)
    return pl.pallas_call(
        combine_kernel,
        out_shape=(out, out),
        grid_spec=pltpu.PrefetchScalarGridSpec(
            num_scalar_prefetch=1,
            grid=(rows_dev // tile,),
            in_specs=[pl.BlockSpec((count, 2, tile, hid), lambda i, ids: (0, 0, i, 0))],
            out_specs=[pl.BlockSpec((experts, tile, hid), lambda i, ids: (0, i, 0))] * 2,
            scratch_shapes=[pltpu.VMEM((2, experts, tile, hid), F32)],
        ),
        compiler_params=pltpu.CompilerParams(vmem_limit_bytes=32 * 1024 * 1024),
    )(ids, pieces)


def body(tokens, grad_out, gate_probs, routes, need_lists, up_weight, down_weight):
    nt, ne = lax.axis_size("tok"), lax.axis_size("exp")
    t, e = lax.axis_index("tok"), lax.axis_index("exp")
    experts = up_weight.shape[0]
    need = need_lists.reshape(ne, ne, nt // ne)
    ids = (jnp.take(need, e, axis=1) - e * experts).reshape(-1)
    sw = jnp.stack([jnp.take(up_weight, ids, axis=0), jnp.take(down_weight, ids, axis=0)], axis=1)
    xs = jnp.stack([tokens.T, grad_out.T])
    slots = 2 * (t // 2) + jnp.arange(2, dtype=jnp.int32)
    p2 = jnp.sum(jnp.where(routes[None] == slots[:, None, None], gate_probs[None], 0.0), axis=2)
    _, _, wout, trecv, gpart = layer(sw, xs, p2[:, None, :], nt, ne)
    token_grads = jnp.sum(trecv.astype(F32), axis=0).astype(BF16).T
    slot_ids = jnp.arange(nt, dtype=jnp.int32)
    hits = routes[None] == slot_ids[:, None, None]
    gate_grads = jnp.sum(jnp.where(hits, gpart.reshape(nt, -1, 1), 0.0), axis=0)
    up_grads, down_grads = combine(ids, wout, experts)
    return (token_grads, gate_grads, up_grads, down_grads)


def solution(mesh):
    split = (P("exp", "tok"), P("exp", "tok"), P("exp", None), P("exp", None))
    weights = P("exp", "tok", None)
    return jax.shard_map(
        body,
        mesh=mesh,
        in_specs=(*split, P(), weights, weights),
        out_specs=(P("exp", "tok"), P("exp", None), weights, weights),
        check_vma=False,
    )
```

```python
import functools

import jax
import jax.numpy as jnp
from jax import lax
from jax.experimental import pallas as pl
from jax.experimental.pallas import tpu as pltpu
from jax.sharding import PartitionSpec as P

MESH = pl.DeviceIdType.MESH
F32 = jnp.float32
BF16 = jnp.bfloat16


def loop(count, step, first=0):
    def run(i, carry):
        step(i)
        return carry

    lax.fori_loop(first, first + count, run, 0)


SIDE = 4
SHIFTS = (
    (2, 2), (1, 2), (3, 2), (2, 0), (0, 2), (1, 0), (3, 0), (0, 0),
    (2, 1), (2, 3), (1, 1), (3, 3), (1, 3), (3, 1), (0, 1), (0, 3),
)
LINE = (1, 3, 2, 0)


def pick(i, values):
    found = jnp.int32(0)
    for n, value in enumerate(values):
        found = jnp.where(i == n, value, found)
    return found


def shift(i):
    return pick(i, [dy for dy, _ in SHIFTS]), pick(i, [dx for _, dx in SHIFTS])


def layer_kernel(
    nt, ne, rows_dev, hid, cols, htile, ntile,
    su, sd, xt, gt, p2,
    relay1, relay2, wout, trecv, gpart,
    xg, ww, pa, pat, dw, cbuf, ring1, ring2, wt, pr, grow,
    s1, r1, sx, tr, sup, sdn, sf, s2, wr, ps, prs, s3, r2, sg, gr, cs, cr, qs, qr, ts, trr, fs, fr,
):
    t = lax.axis_index("tok")
    e = lax.axis_index("exp")
    z, k = lax.div(e, 2), lax.rem(e, 2)
    y, x = lax.div(t, SIDE), lax.rem(t, SIDE)
    q, h = lax.div(t, 2), lax.rem(t, 2)
    nz, ny = ne // 2, nt // SIDE
    sibling = 2 * z + 1 - k
    column_core = 2 * z + h
    above = lax.rem(y + 1, ny) * SIDE + x
    below = lax.rem(y + ny - 1, ny) * SIDE + x

    def remote(src, dst, send, recv, tok, ex):
        return pltpu.make_async_remote_copy(
            src_ref=src, dst_ref=dst, send_sem=send, recv_sem=recv,
            device_id=(tok, ex), device_id_type=MESH,
        )

    def push(src, dst, send, recv, tok, ex):
        own = jnp.logical_and(tok == t, ex == e)

        @pl.when(own)
        def _():
            pltpu.make_async_copy(src, dst, recv).start()

        @pl.when(jnp.logical_not(own))
        def _():
            remote(src, dst, send, recv, tok, ex).start()

    def sent(src, dst, send, recv, tok, ex):
        @pl.when(jnp.logical_not(jnp.logical_and(tok == t, ex == e)))
        def _():
            remote(src, dst, send, recv, tok, ex).wait_send()

    def landed(dst, recv):
        pltpu.make_async_copy(dst, dst, recv).wait()

    def place_of(tok):
        return lax.rem(tok, 2) * ne + lax.div(tok, 2)

    def rows(block):
        return pl.ds(pl.multiple_of(place_of(block) * rows_dev, rows_dev), rows_dev)

    def pair_rows(row, core):
        return pl.ds(pl.multiple_of((core * ne + 2 * row) * rows_dev, 2 * rows_dev), 2 * rows_dev)

    def target(i):
        dy, dx = shift(i)
        return lax.rem(y + dy, ny) * SIDE + lax.rem(x + dx, SIDE)

    def origin(i):
        dy, dx = shift(i)
        return lax.rem(y + ny - dy, ny) * SIDE + lax.rem(x + SIDE - dx, SIDE)

    barrier = pltpu.get_barrier_semaphore()

    def greet_plane(i):
        tok, ex = lax.div(i, 2), 2 * z + lax.rem(i, 2)

        @pl.when(jnp.logical_not(jnp.logical_and(tok == t, ex == e)))
        def _():
            pl.semaphore_signal(barrier, inc=1, device_id=(tok, ex), device_id_type=MESH)

    def greet_line(ex):
        @pl.when(lax.div(ex, 2) != z)
        def _():
            pl.semaphore_signal(barrier, inc=1, device_id=(t, ex), device_id_type=MESH)

    loop(2 * nt, greet_plane)
    loop(ne, greet_line)
    pl.semaphore_wait(barrier, 2 * nt - 1 + ne - 2)

    def token_part(a, block):
        return xg.at[a, rows(block), :]

    def row_copy(a, i):
        src = (xt, gt)[a]
        return (
            src, token_part(a, t), sx.at[2 * i + a], tr.at[2 * t + a],
            y * SIDE + k + 2 * i, column_core,
        )

    def ring_copy(a, block, sem, tok):
        part = token_part(a, block)
        return remote(part, part, sem, tr.at[2 * block + a], tok, e)

    def twin_copy(a, block, i):
        part = token_part(a, block)
        return remote(part, part, sf.at[2 * i + a], tr.at[2 * block + a], t, sibling)

    def row_block(dy, w):
        return lax.rem(y + dy, ny) * SIDE + k + 2 * w

    def line_copy(a, hs, i):
        half, core = lax.rem(x + hs, 2), lax.rem(i, 2)
        plane = lax.rem(z + pick(lax.div(i, 2), LINE), nz)
        piece = (2 * plane + half) * 2 + core
        m = half * ne + e
        src = (su, sd)[a]
        n = 2 * (ne * hs + i) + a
        return (src.at[piece], relay1.at[m, a], s1.at[n], r1.at[2 * m + a], t, 2 * plane + core)

    def plane_copy(a, i):
        tok = target(i)
        return (relay1.at[place_of(tok), a], ww.at[a, rows(t), :], s2.at[2 * i + a], wr.at[2 * t + a], tok, e)

    prob_copy = remote(p2.at[1 - k], pr, ps, prs, t, sibling)
    prob_copy.start()
    for a in range(2):
        loop(2, lambda i: push(*row_copy(a, i)))

    for hs in range(2):
        for a in range(2):
            loop(ne, lambda i: push(*line_copy(a, hs, i)))

    def forward_row(i):
        for a in range(2):
            block = row_block(0, i)
            landed(token_part(a, block), tr.at[2 * block + a])
            twin_copy(a, block, i).start()
            ring_copy(a, block, sup.at[2 * i + a], above).start()
            ring_copy(a, block, sdn.at[2 * i + a], below).start()

    loop(2, forward_row)

    def forward_ring():
        for a in range(2):
            lower, upper = row_block(ny - 1, 0), row_block(1, 1)
            landed(token_part(a, lower), tr.at[2 * lower + a])
            ring_copy(a, lower, sup.at[4 + a], above).start()
            twin_copy(a, lower, 2).start()
            landed(token_part(a, upper), tr.at[2 * upper + a])
            ring_copy(a, upper, sdn.at[4 + a], below).start()
            twin_copy(a, upper, 3).start()

    def forward_weights(hs, a):
        def step(i):
            m = place_of(target(i))
            landed(relay1.at[m, a], r1.at[2 * m + a])
            push(*plane_copy(a, i))

        loop(ne, step, hs * ne)

    forward_weights(0, 0)
    forward_weights(0, 1)
    forward_ring()
    forward_weights(1, 0)
    forward_weights(1, 1)

    late = ((ny - 1, 1), (1, 0), (2, 0), (2, 1))
    for n, (dy, w) in enumerate(late):
        for a in range(2):
            block = row_block(dy, w)
            landed(token_part(a, block), tr.at[2 * block + a])
            twin_copy(a, block, 4 + n).start()

    def take_tokens(i):
        block = 2 * i + 1 - k
        for a in range(2):
            landed(token_part(a, block), tr.at[2 * block + a])

    loop(nt // 2, take_tokens)
    for a in range(2):
        loop(nt, lambda i: landed(ww.at[a, rows(i), :], wr.at[2 * i + a]))
    prob_copy.wait()
    for a in range(2):
        loop(2, lambda i: sent(*row_copy(a, i)))
        for hs in range(2):
            loop(ne, lambda i: sent(*line_copy(a, hs, i)))
        loop(nt, lambda i: sent(*plane_copy(a, i)))
        for i in range(3):
            ring_copy(a, t, sup.at[2 * i + a], above).wait_send()
            ring_copy(a, t, sdn.at[2 * i + a], below).wait_send()
        loop(nt // 2, lambda i: twin_copy(a, t, i).wait_send())

    grow[...] = jnp.zeros_like(grow)
    mine = jnp.where(k == h, 1.0, 0.0).astype(F32)

    def hidden(hi):
        units = pl.ds(pl.multiple_of(hi * htile, htile), htile)
        wt[0] = ww[0, :, units].T
        wt[1] = ww[1, :, units].T

        def strip(ni):
            lanes = pl.ds(pl.multiple_of(ni * ntile, ntile), ntile)
            pre = jnp.dot(wt[0], xg[0, :, lanes], preferred_element_type=F32)
            hg = jnp.dot(wt[1], xg[1, :, lanes], preferred_element_type=F32)
            prob = p2[k, :, lanes] * mine + pr[:, lanes] * (1.0 - mine)
            sig = 1.0 / (1.0 + jnp.exp(-pre))
            act = (pre * sig).astype(BF16).astype(F32)
            slope = sig * (1.0 + pre * (1.0 - sig))
            grad = (prob * hg * slope).astype(BF16)
            pa[units, lanes] = grad
            pat[0, lanes, units] = grad.T
            pat[1, lanes, units] = (prob * act).astype(BF16).T
            grow[:, lanes] = grow[:, lanes] + jnp.sum(act * hg, axis=0, keepdims=True)

        loop(cols // ntile, strip)

    loop(hid // htile, hidden)

    def gate_copy(i):
        j = 2 * q + k
        return (grow, gpart.at[j], sg.at[i], gr.at[j], target(i), column_core)

    def grad_copy(a, i):
        block = target(i)
        m = h * ne + q
        src = ww.at[1, rows(block), :] if a == 0 else dw.at[rows(block), :]
        return (src, relay2.at[m, a], s3.at[2 * i + a], r2.at[2 * m + a], block, e)

    def weight_grads(i):
        part = rows(target(i))
        ww[1, part, :] = jnp.dot(xg[0, part, :], pat[0], preferred_element_type=F32).astype(BF16)
        push(*grad_copy(0, i))
        dw[part, :] = jnp.dot(xg[1, part, :], pat[1], preferred_element_type=F32).astype(BF16)
        push(*grad_copy(1, i))

    def owner_copy(i):
        tok = origin(i)
        piece = (2 * z + lax.rem(tok, 2)) * 2 + k
        return (relay2.at[place_of(tok)], wout.at[piece], fs.at[i], fr.at[piece], t, lax.div(tok, 2))

    def forward_grads(i):
        m = place_of(origin(i))
        for a in range(2):
            landed(relay2.at[m, a], r2.at[2 * m + a])
        push(*owner_copy(i))

    def row_at(dy):
        return lax.rem(y + dy, ny)

    def pair_copy(n, dy):
        row = row_at(dy)
        return remote(xg.at[0, pair_rows(row, 1 - k), :], cbuf.at[row], cs.at[n], cr.at[row], t, sibling)

    def give(n, dy):
        part = pair_rows(row_at(dy), 1 - k)
        xg[0, part, :] = jnp.dot(ww[0, part, :], pa[...], preferred_element_type=F32).astype(BF16)
        pair_copy(n, dy).start()

    def half_rows(row, w):
        return rows(row * SIDE + k + 2 * w)

    def keep(dy, added):
        row = row_at(dy)
        landed(cbuf.at[row], cr.at[row])
        for w in range(2):
            part = half_rows(row, w)
            total = jnp.dot(ww[0, part, :], pa[...], preferred_element_type=F32)
            total = total + cbuf[row, w * rows_dev:(w + 1) * rows_dev, :].astype(F32)
            for term in added[w]:
                total = total + term[...].astype(F32)
            xg[0, part, :] = total.astype(BF16)

    def far_copies():
        row = row_at(2)
        return (
            remote(xg.at[0, half_rows(row, 0), :], ring1.at[1], qs.at[0], qr.at[1], below, e),
            remote(xg.at[0, half_rows(row, 1), :], ring1.at[0], qs.at[1], qr.at[0], above, e),
        )

    def near_copy(n):
        src = xg.at[0, pair_rows(row_at((1, ny - 1)[n]), k), :]
        return remote(src, ring2.at[n], qs.at[2 + n], qr.at[2 + n], (above, below)[n], e)

    def row_owner(w):
        return (
            xg.at[0, half_rows(y, w), :], trecv.at[lax.div(x, 2)], ts.at[w], trr.at[lax.div(x, 2)],
            y * SIDE + k + 2 * w, column_core,
        )

    gives = (2, 1, ny - 1, 0)
    quarter = nt // 4
    loop(nt, weight_grads)
    loop(nt, lambda i: push(*gate_copy(i)))
    for n, dy in enumerate(gives):
        give(n, dy)
    keep(2, ((), ()))
    for copy in far_copies():
        copy.start()
    loop(quarter, forward_grads)
    landed(ring1.at[0], qr.at[0])
    keep(1, ((), (ring1.at[0],)))
    near_copy(0).start()
    loop(quarter, forward_grads, quarter)
    landed(ring1.at[1], qr.at[1])
    keep(ny - 1, ((ring1.at[1],), ()))
    near_copy(1).start()
    loop(quarter, forward_grads, 2 * quarter)
    for n in range(2):
        landed(ring2.at[n], qr.at[2 + n])
    both = [[ring2.at[n, pl.ds(w * rows_dev, rows_dev), :] for n in range(2)] for w in range(2)]
    keep(0, both)
    for w in range(2):
        push(*row_owner(w))
    loop(quarter, forward_grads, 3 * quarter)

    loop(2 * ne, lambda i: landed(wout.at[i], fr.at[i]))
    loop(2, lambda i: landed(trecv.at[i], trr.at[i]))
    loop(nt, lambda i: landed(gpart.at[i], gr.at[i]))
    loop(nt, lambda i: sent(*gate_copy(i)))
    for a in range(2):
        loop(nt, lambda i: sent(*grad_copy(a, i)))
    for n, dy in enumerate(gives):
        pair_copy(n, dy).wait_send()
    for copy in (*far_copies(), near_copy(0), near_copy(1)):
        copy.wait_send()
    for w in range(2):
        sent(*row_owner(w))
    loop(nt, lambda i: sent(*owner_copy(i)))


def layer(su, sd, xt, gt, p2, nt, ne):
    pieces, rows_dev, hid = su.shape
    cols = xt.shape[1]
    width = nt * rows_dev
    ny = nt // SIDE
    htile, ntile = min(256, hid), min(512, cols)
    dma = pltpu.SemaphoreType.DMA
    anywhere = pl.BlockSpec(memory_space=pl.ANY)
    relay = jax.ShapeDtypeStruct((pieces, 2, rows_dev, hid), BF16)
    counts = (4 * ne, 4 * ne, 4, 2 * nt, 6, 6, nt, 2 * nt, 2 * nt)
    counts_back = (2 * nt, 4 * ne, nt, nt, ny, ny, 4, 4, 2, 2, nt, 2 * ne)
    return pl.pallas_call(
        functools.partial(layer_kernel, nt, ne, rows_dev, hid, cols, htile, ntile),
        out_shape=(
            relay,
            relay,
            relay,
            jax.ShapeDtypeStruct((2, rows_dev, cols), BF16),
            jax.ShapeDtypeStruct((nt, 1, cols), F32),
        ),
        in_specs=[anywhere] * 4 + [pl.BlockSpec(memory_space=pltpu.VMEM)],
        out_specs=(anywhere,) * 5,
        scratch_shapes=[
            pltpu.VMEM((2, width, cols), BF16),
            pltpu.VMEM((2, width, hid), BF16),
            pltpu.VMEM((hid, cols), BF16),
            pltpu.VMEM((2, cols, hid), BF16),
            pltpu.VMEM((width, hid), BF16),
            pltpu.VMEM((ny, 2 * rows_dev, cols), BF16),
            pltpu.VMEM((2, rows_dev, cols), BF16),
            pltpu.VMEM((2, 2 * rows_dev, cols), BF16),
            pltpu.VMEM((2, htile, width), BF16),
            pltpu.VMEM((1, cols), F32),
            pltpu.VMEM((1, cols), F32),
            *[dma((count,)) for count in counts],
            dma,
            dma,
            *[dma((count,)) for count in counts_back],
        ],
        compiler_params=pltpu.CompilerParams(
            collective_id=0, has_side_effects=True, vmem_limit_bytes=60 * 1024 * 1024
        ),
        cost_estimate=pl.CostEstimate(
            flops=10 * width * hid * cols, bytes_accessed=64 << 20, transcendentals=hid * cols
        ),
    )(su, sd, xt, gt, p2)


def combine_kernel(ids, pieces, up_out, down_out, total):
    total[...] = jnp.zeros_like(total)
    for n in range(pieces.shape[0]):
        expert = ids[n]
        for a in range(2):
            total[a, expert] = total[a, expert] + pieces[n, a].astype(F32)
    up_out[...] = total[0].astype(BF16)
    down_out[...] = total[1].astype(BF16)


def combine(ids, pieces, experts):
    count, _, rows_dev, hid = pieces.shape
    tile = 32 if rows_dev % 32 == 0 else 16
    out = jax.ShapeDtypeStruct((experts, rows_dev, hid), BF16)
    return pl.pallas_call(
        combine_kernel,
        out_shape=(out, out),
        grid_spec=pltpu.PrefetchScalarGridSpec(
            num_scalar_prefetch=1,
            grid=(rows_dev // tile,),
            in_specs=[pl.BlockSpec((count, 2, tile, hid), lambda i, ids: (0, 0, i, 0))],
            out_specs=[pl.BlockSpec((experts, tile, hid), lambda i, ids: (0, i, 0))] * 2,
            scratch_shapes=[pltpu.VMEM((2, experts, tile, hid), F32)],
        ),
        compiler_params=pltpu.CompilerParams(vmem_limit_bytes=32 * 1024 * 1024),
    )(ids, pieces)


def body(tokens, grad_out, gate_probs, routes, need_lists, up_weight, down_weight):
    nt, ne = lax.axis_size("tok"), lax.axis_size("exp")
    t, e = lax.axis_index("tok"), lax.axis_index("exp")
    experts = up_weight.shape[0]
    need = need_lists.reshape(ne, ne, nt // ne)
    ids = (jnp.take(need, e, axis=1) - e * experts).reshape(-1)
    su = up_weight.at[ids].get(mode="promise_in_bounds")
    sd = down_weight.at[ids].get(mode="promise_in_bounds")
    slots = 2 * (t // 2) + jnp.arange(2, dtype=jnp.int32)
    p2 = jnp.sum(jnp.where(routes[None] == slots[:, None, None], gate_probs[None], 0.0), axis=2)
    _, _, wout, trecv, gpart = layer(su, sd, tokens.T, grad_out.T, p2[:, None, :], nt, ne)
    token_grads = jnp.sum(trecv.astype(F32), axis=0).astype(BF16).T
    slot_ids = jnp.arange(nt, dtype=jnp.int32)
    hits = routes[None] == slot_ids[:, None, None]
    gate_grads = jnp.sum(jnp.where(hits, gpart.reshape(nt, -1, 1), 0.0), axis=0)
    up_grads, down_grads = combine(ids, wout, experts)
    return (token_grads, gate_grads, up_grads, down_grads)


def solution(mesh):
    split = (P("exp", "tok"), P("exp", "tok"), P("exp", None), P("exp", None))
    weights = P("exp", "tok", None)
    return jax.shard_map(
        body,
        mesh=mesh,
        in_specs=(*split, P(), weights, weights),
        out_specs=(P("exp", "tok"), P("exp", None), weights, weights),
        check_vma=False,
    )
```

```python
import functools

import jax
import jax.numpy as jnp
from jax import lax
from jax.experimental import pallas as pl
from jax.experimental.pallas import tpu as pltpu
from jax.sharding import PartitionSpec as P

MESH = pl.DeviceIdType.MESH
F32 = jnp.float32
BF16 = jnp.bfloat16


def loop(count, step, first=0):
    def run(i, carry):
        step(i)
        return carry

    lax.fori_loop(first, first + count, run, 0)


SIDE = 4
SHIFTS = (
    (2, 2), (1, 2), (3, 2), (2, 0), (0, 2), (1, 0), (3, 0), (0, 0),
    (2, 1), (2, 3), (1, 1), (3, 3), (1, 3), (3, 1), (0, 1), (0, 3),
)
LINE = (1, 3, 2, 0)
PARTS = 3


def pick(i, values):
    found = jnp.int32(0)
    for n, value in enumerate(values):
        found = jnp.where(i == n, value, found)
    return found


def shift(i):
    return pick(i, [dy for dy, _ in SHIFTS]), pick(i, [dx for _, dx in SHIFTS])


def layer_kernel(
    nt, ne, rows_dev, hid, cols, htile, ntile,
    sw, xt, gt, p2,
    relay1, relay2, wout, trecv, gpart,
    xg, ww, pa, pat, dw, cbuf, ring1, ring2, wt, pr, grow,
    s1, r1, sx, tr, sup, sdn, sf, s2, wr, ps, prs, s3, r2, sg, gr, cs, cr, qs, qr, ts, trr, fs, fr,
):
    t = lax.axis_index("tok")
    e = lax.axis_index("exp")
    z, k = lax.div(e, 2), lax.rem(e, 2)
    y, x = lax.div(t, SIDE), lax.rem(t, SIDE)
    q, h = lax.div(t, 2), lax.rem(t, 2)
    nz, ny = ne // 2, nt // SIDE
    sibling = 2 * z + 1 - k
    column_core = 2 * z + h
    above = lax.rem(y + 1, ny) * SIDE + x
    below = lax.rem(y + ny - 1, ny) * SIDE + x

    def remote(src, dst, send, recv, tok, ex):
        return pltpu.make_async_remote_copy(
            src_ref=src, dst_ref=dst, send_sem=send, recv_sem=recv,
            device_id=(tok, ex), device_id_type=MESH,
        )

    def push(src, dst, send, recv, tok, ex):
        own = jnp.logical_and(tok == t, ex == e)

        @pl.when(own)
        def _():
            pltpu.make_async_copy(src, dst, recv).start()

        @pl.when(jnp.logical_not(own))
        def _():
            remote(src, dst, send, recv, tok, ex).start()

    def sent(src, dst, send, recv, tok, ex):
        @pl.when(jnp.logical_not(jnp.logical_and(tok == t, ex == e)))
        def _():
            remote(src, dst, send, recv, tok, ex).wait_send()

    def landed(dst, recv):
        pltpu.make_async_copy(dst, dst, recv).wait()

    def place_of(tok):
        return lax.rem(tok, 2) * ne + lax.div(tok, 2)

    def rows(block):
        return pl.ds(pl.multiple_of(place_of(block) * rows_dev, rows_dev), rows_dev)

    def pair_rows(row, core):
        return pl.ds(pl.multiple_of((core * ne + 2 * row) * rows_dev, 2 * rows_dev), 2 * rows_dev)

    def target(i):
        dy, dx = shift(i)
        return lax.rem(y + dy, ny) * SIDE + lax.rem(x + dx, SIDE)

    def origin(i):
        dy, dx = shift(i)
        return lax.rem(y + ny - dy, ny) * SIDE + lax.rem(x + SIDE - dx, SIDE)

    barrier = pltpu.get_barrier_semaphore()

    def greet_plane(i):
        tok, ex = lax.div(i, 2), 2 * z + lax.rem(i, 2)

        @pl.when(jnp.logical_not(jnp.logical_and(tok == t, ex == e)))
        def _():
            pl.semaphore_signal(barrier, inc=1, device_id=(tok, ex), device_id_type=MESH)

    def greet_line(ex):
        @pl.when(lax.div(ex, 2) != z)
        def _():
            pl.semaphore_signal(barrier, inc=1, device_id=(t, ex), device_id_type=MESH)

    loop(2 * nt, greet_plane)
    loop(ne, greet_line)
    pl.semaphore_wait(barrier, 2 * nt - 1 + ne - 2)

    def token_part(a, block):
        return xg.at[a, rows(block), :]

    def row_copy(a, i):
        src = (xt, gt)[a]
        return (
            src, token_part(a, t), sx.at[2 * i + a], tr.at[2 * t + a],
            y * SIDE + k + 2 * i, column_core,
        )

    def ring_copy(a, block, sem, tok):
        part = token_part(a, block)
        return remote(part, part, sem, tr.at[2 * block + a], tok, e)

    def twin_copy(a, block, i):
        part = token_part(a, block)
        return remote(part, part, sf.at[2 * i + a], tr.at[2 * block + a], t, sibling)

    def row_block(dy, w):
        return lax.rem(y + dy, ny) * SIDE + k + 2 * w

    def line_copy(s, i):
        hs, j = lax.div(i, ne), lax.rem(i, ne)
        half, core = lax.rem(x + hs, 2), lax.rem(j, 2)
        plane = lax.rem(z + pick(lax.div(j, 2), LINE), nz)
        piece = (2 * plane + half) * 2 + core
        m = half * ne + e
        return (
            sw.at[piece, s], relay1.at[m, s], s1.at[2 * ne * s + i], r1.at[2 * ne * s + m], t, 2 * plane + core,
        )

    def plane_copy(s, i):
        tok = target(i)
        return (
            relay1.at[place_of(tok), s], ww.at[s, :, rows(t), :], s2.at[nt * s + i], wr.at[nt * s + t], tok, e,
        )

    prob_copy = remote(p2.at[1 - k], pr, ps, prs, t, sibling)
    prob_copy.start()
    for a in range(2):
        loop(2, lambda i: push(*row_copy(a, i)))

    def send_line(s):
        loop(2 * ne, lambda i: push(*line_copy(s, i)))

    send_line(0)
    send_line(1)

    def forward_row(i):
        for a in range(2):
            block = row_block(0, i)
            landed(token_part(a, block), tr.at[2 * block + a])
            twin_copy(a, block, i).start()
            ring_copy(a, block, sup.at[2 * i + a], above).start()
            ring_copy(a, block, sdn.at[2 * i + a], below).start()

    def forward_ring():
        for a in range(2):
            lower, upper = row_block(ny - 1, 0), row_block(1, 1)
            landed(token_part(a, lower), tr.at[2 * lower + a])
            ring_copy(a, lower, sup.at[4 + a], above).start()
            twin_copy(a, lower, 2).start()
            landed(token_part(a, upper), tr.at[2 * upper + a])
            ring_copy(a, upper, sdn.at[4 + a], below).start()
            twin_copy(a, upper, 3).start()

    def forward_weights(s):
        def step(i):
            m = place_of(target(i))
            landed(relay1.at[m, s], r1.at[2 * ne * s + m])
            push(*plane_copy(s, i))

        loop(nt, step)

    loop(2, forward_row)
    forward_weights(0)
    send_line(2)
    forward_ring()
    forward_weights(1)
    late = ((ny - 1, 1), (1, 0), (2, 0), (2, 1))
    for n, (dy, w) in enumerate(late):
        for a in range(2):
            block = row_block(dy, w)
            landed(token_part(a, block), tr.at[2 * block + a])
            twin_copy(a, block, 4 + n).start()

    forward_weights(2)

    def take_tokens(i):
        block = 2 * i + 1 - k
        for a in range(2):
            landed(token_part(a, block), tr.at[2 * block + a])

    loop(nt // 2, take_tokens)
    prob_copy.wait()

    grow[...] = jnp.zeros_like(grow)
    mine = jnp.where(k == h, 1.0, 0.0).astype(F32)

    def hidden(s):
        units = pl.ds(s * htile, htile)
        loop(nt, lambda i: landed(ww.at[s, :, rows(i), :], wr.at[nt * s + i]))
        wt[0] = ww[s, 0].T
        wt[1] = ww[s, 1].T

        def strip(ni):
            lanes = pl.ds(pl.multiple_of(ni * ntile, ntile), ntile)
            pre = jnp.dot(wt[0], xg[0, :, lanes], preferred_element_type=F32)
            hg = jnp.dot(wt[1], xg[1, :, lanes], preferred_element_type=F32)
            prob = p2[k, :, lanes] * mine + pr[:, lanes] * (1.0 - mine)
            sig = 1.0 / (1.0 + jnp.exp(-pre))
            act = (pre * sig).astype(BF16).astype(F32)
            slope = sig * (1.0 + pre * (1.0 - sig))
            grad = (prob * hg * slope).astype(BF16)
            pa[units, lanes] = grad
            pat[0, lanes, :] = grad.T
            pat[1, lanes, :] = (prob * act).astype(BF16).T
            grow[:, lanes] = grow[:, lanes] + jnp.sum(act * hg, axis=0, keepdims=True)

        loop(cols // ntile, strip)

    def gate_copy(i):
        j = 2 * q + k
        return (grow, gpart.at[j], sg.at[i], gr.at[j], target(i), column_core)

    def grad_copy(s, i):
        block = target(i)
        m = h * ne + q
        return (dw.at[s, :, rows(block), :], relay2.at[m, s], s3.at[nt * s + i], r2.at[2 * ne * s + m], block, e)

    def weight_grads(s):
        def step(i):
            part = rows(target(i))
            for a in range(2):
                dw[s, a, part, :] = jnp.dot(xg[a, part, :], pat[a], preferred_element_type=F32).astype(BF16)
            push(*grad_copy(s, i))

        loop(nt, step)

    def owner_copy(s, i):
        tok = origin(i)
        piece = (2 * z + lax.rem(tok, 2)) * 2 + k
        return (
            relay2.at[place_of(tok), s], wout.at[piece, s], fs.at[nt * s + i], fr.at[2 * ne * s + piece],
            t, lax.div(tok, 2),
        )

    def forward_grads(s, count=nt, first=0):
        def step(i):
            m = place_of(origin(i))
            landed(relay2.at[m, s], r2.at[2 * ne * s + m])
            push(*owner_copy(s, i))

        loop(count, step, first)

    def row_at(dy):
        return lax.rem(y + dy, ny)

    def token_part_grads(part):
        weights = jnp.concatenate([ww[s, 0, part, :] for s in range(PARTS)], axis=1)
        return jnp.dot(weights, pa[...], preferred_element_type=F32)

    def pair_copy(n, dy):
        row = row_at(dy)
        return remote(xg.at[0, pair_rows(row, 1 - k), :], cbuf.at[row], cs.at[n], cr.at[row], t, sibling)

    def give(n, dy):
        part = pair_rows(row_at(dy), 1 - k)
        xg[0, part, :] = token_part_grads(part).astype(BF16)
        pair_copy(n, dy).start()

    def half_rows(row, w):
        return rows(row * SIDE + k + 2 * w)

    def keep(dy, added):
        row = row_at(dy)
        landed(cbuf.at[row], cr.at[row])
        for w in range(2):
            part = half_rows(row, w)
            total = token_part_grads(part)
            total = total + cbuf[row, w * rows_dev:(w + 1) * rows_dev, :].astype(F32)
            for term in added[w]:
                total = total + term[...].astype(F32)
            xg[0, part, :] = total.astype(BF16)

    def far_copies():
        row = row_at(2)
        return (
            remote(xg.at[0, half_rows(row, 0), :], ring1.at[1], qs.at[0], qr.at[1], below, e),
            remote(xg.at[0, half_rows(row, 1), :], ring1.at[0], qs.at[1], qr.at[0], above, e),
        )

    def near_copy(n):
        src = xg.at[0, pair_rows(row_at((1, ny - 1)[n]), k), :]
        return remote(src, ring2.at[n], qs.at[2 + n], qr.at[2 + n], (above, below)[n], e)

    def row_owner(w):
        return (
            xg.at[0, half_rows(y, w), :], trecv.at[lax.div(x, 2)], ts.at[w], trr.at[lax.div(x, 2)],
            y * SIDE + k + 2 * w, column_core,
        )

    gives = (2, 1, ny - 1, 0)
    quarter = nt // 4
    last = PARTS - 1
    for s in range(PARTS):
        hidden(s)
        weight_grads(s)
        if s == last:
            break
    forward_grads(0)
    loop(nt, lambda i: push(*gate_copy(i)))
    for a in range(2):
        for i in range(3):
            ring_copy(a, t, sup.at[2 * i + a], above).wait_send()
            ring_copy(a, t, sdn.at[2 * i + a], below).wait_send()
        loop(nt // 2, lambda i: twin_copy(a, t, i).wait_send())
    for n, dy in enumerate(gives):
        give(n, dy)
    keep(2, ((), ()))
    for copy in far_copies():
        copy.start()
    forward_grads(last - 1)
    landed(ring1.at[0], qr.at[0])
    keep(1, ((), (ring1.at[0],)))
    near_copy(0).start()
    forward_grads(last, quarter)
    landed(ring1.at[1], qr.at[1])
    keep(ny - 1, ((ring1.at[1],), ()))
    near_copy(1).start()
    forward_grads(last, 2 * quarter, quarter)
    for n in range(2):
        landed(ring2.at[n], qr.at[2 + n])
    both = [[ring2.at[n, pl.ds(w * rows_dev, rows_dev), :] for n in range(2)] for w in range(2)]
    keep(0, both)
    for w in range(2):
        push(*row_owner(w))
    forward_grads(last, quarter, 3 * quarter)

    for s in range(PARTS):
        loop(2 * ne, lambda i: landed(wout.at[i, s], fr.at[2 * ne * s + i]))
    loop(2, lambda i: landed(trecv.at[i], trr.at[i]))
    loop(nt, lambda i: landed(gpart.at[i], gr.at[i]))
    loop(nt, lambda i: sent(*gate_copy(i)))
    for a in range(2):
        loop(2, lambda i: sent(*row_copy(a, i)))
    for s in range(PARTS):
        loop(2 * ne, lambda i: sent(*line_copy(s, i)))
        loop(nt, lambda i: sent(*plane_copy(s, i)))
        loop(nt, lambda i: sent(*grad_copy(s, i)))
        loop(nt, lambda i: sent(*owner_copy(s, i)))
    for n, dy in enumerate(gives):
        pair_copy(n, dy).wait_send()
    for copy in (*far_copies(), near_copy(0), near_copy(1)):
        copy.wait_send()
    for w in range(2):
        sent(*row_owner(w))


def layer(sw, xt, gt, p2, nt, ne):
    _, _, _, rows_dev, htile = sw.shape
    hid = PARTS * htile
    cols = xt.shape[1]
    width = nt * rows_dev
    ny = nt // SIDE
    ntile = min(512, cols)
    dma = pltpu.SemaphoreType.DMA
    anywhere = pl.BlockSpec(memory_space=pl.ANY)
    relay = jax.ShapeDtypeStruct(sw.shape, BF16)
    counts = (6 * ne, 6 * ne, 4, 2 * nt, 6, 6, nt, 3 * nt, 3 * nt)
    counts_back = (3 * nt, 6 * ne, nt, nt, ny, ny, 4, 4, 2, 2, 3 * nt, 6 * ne)
    return pl.pallas_call(
        functools.partial(layer_kernel, nt, ne, rows_dev, hid, cols, htile, ntile),
        out_shape=(
            relay,
            relay,
            relay,
            jax.ShapeDtypeStruct((2, rows_dev, cols), BF16),
            jax.ShapeDtypeStruct((nt, 1, cols), F32),
        ),
        in_specs=[anywhere] * 3 + [pl.BlockSpec(memory_space=pltpu.VMEM)],
        out_specs=(anywhere,) * 5,
        scratch_shapes=[
            pltpu.VMEM((2, width, cols), BF16),
            pltpu.VMEM((PARTS, 2, width, htile), BF16),
            pltpu.VMEM((hid, cols), BF16),
            pltpu.VMEM((2, cols, htile), BF16),
            pltpu.VMEM((PARTS, 2, width, htile), BF16),
            pltpu.VMEM((ny, 2 * rows_dev, cols), BF16),
            pltpu.VMEM((2, rows_dev, cols), BF16),
            pltpu.VMEM((2, 2 * rows_dev, cols), BF16),
            pltpu.VMEM((2, htile, width), BF16),
            pltpu.VMEM((1, cols), F32),
            pltpu.VMEM((1, cols), F32),
            *[dma((count,)) for count in counts],
            dma,
            dma,
            *[dma((count,)) for count in counts_back],
        ],
        compiler_params=pltpu.CompilerParams(
            collective_id=0, has_side_effects=True, vmem_limit_bytes=60 * 1024 * 1024
        ),
        cost_estimate=pl.CostEstimate(
            flops=10 * width * hid * cols, bytes_accessed=64 << 20, transcendentals=hid * cols
        ),
    )(sw, xt, gt, p2)


def take_kernel(ids, up, down, out):
    htile = out.shape[-1]
    for s in range(PARTS):
        for a, weight in enumerate((up, down)):
            out[0, s, a] = weight[0, :, s * htile:(s + 1) * htile]


def take(ids, up_weight, down_weight):
    _, rows_dev, hid = up_weight.shape
    count = ids.shape[0]
    block = (1, PARTS, 2, rows_dev, hid // PARTS)
    return pl.pallas_call(
        take_kernel,
        out_shape=jax.ShapeDtypeStruct((count, *block[1:]), BF16),
        grid_spec=pltpu.PrefetchScalarGridSpec(
            num_scalar_prefetch=1,
            grid=(count,),
            in_specs=[pl.BlockSpec((1, rows_dev, hid), lambda i, ids: (ids[i], 0, 0))] * 2,
            out_specs=pl.BlockSpec(block, lambda i, ids: (i, 0, 0, 0, 0)),
        ),
    )(ids, up_weight, down_weight)


def combine_kernel(ids, pieces, up_out, down_out, total):
    htile = pieces.shape[-1]
    total[...] = jnp.zeros_like(total)
    for n in range(pieces.shape[0]):
        expert = ids[n]
        for s in range(PARTS):
            units = slice(s * htile, (s + 1) * htile)
            for a in range(2):
                total[a, expert, :, units] = total[a, expert, :, units] + pieces[n, s, a].astype(F32)
    up_out[...] = total[0].astype(BF16)
    down_out[...] = total[1].astype(BF16)


def combine(ids, pieces, experts):
    count, parts, _, rows_dev, htile = pieces.shape
    hid = parts * htile
    tile = 32 if rows_dev % 32 == 0 else 16
    out = jax.ShapeDtypeStruct((experts, rows_dev, hid), BF16)
    return pl.pallas_call(
        combine_kernel,
        out_shape=(out, out),
        grid_spec=pltpu.PrefetchScalarGridSpec(
            num_scalar_prefetch=1,
            grid=(rows_dev // tile,),
            in_specs=[pl.BlockSpec((count, parts, 2, tile, htile), lambda i, ids: (0, 0, 0, i, 0))],
            out_specs=[pl.BlockSpec((experts, tile, hid), lambda i, ids: (0, i, 0))] * 2,
            scratch_shapes=[pltpu.VMEM((2, experts, tile, hid), F32)],
        ),
        compiler_params=pltpu.CompilerParams(vmem_limit_bytes=32 * 1024 * 1024),
    )(ids, pieces)


def body(tokens, grad_out, gate_probs, routes, need_lists, up_weight, down_weight):
    nt, ne = lax.axis_size("tok"), lax.axis_size("exp")
    t, e = lax.axis_index("tok"), lax.axis_index("exp")
    experts = up_weight.shape[0]
    need = need_lists.reshape(ne, ne, nt // ne)
    ids = (jnp.take(need, e, axis=1) - e * experts).reshape(-1)
    sw = take(ids, up_weight, down_weight)
    slots = 2 * (t // 2) + jnp.arange(2, dtype=jnp.int32)
    p2 = jnp.sum(jnp.where(routes[None] == slots[:, None, None], gate_probs[None], 0.0), axis=2)
    _, _, wout, trecv, gpart = layer(sw, tokens.T, grad_out.T, p2[:, None, :], nt, ne)
    token_grads = jnp.sum(trecv.astype(F32), axis=0).astype(BF16).T
    slot_ids = jnp.arange(nt, dtype=jnp.int32)
    hits = routes[None] == slot_ids[:, None, None]
    gate_grads = jnp.sum(jnp.where(hits, gpart.reshape(nt, -1, 1), 0.0), axis=0)
    up_grads, down_grads = combine(ids, wout, experts)
    return (token_grads, gate_grads, up_grads, down_grads)


def solution(mesh):
    split = (P("exp", "tok"), P("exp", "tok"), P("exp", None), P("exp", None))
    weights = P("exp", "tok", None)
    return jax.shard_map(
        body,
        mesh=mesh,
        in_specs=(*split, P(), weights, weights),
        out_specs=(P("exp", "tok"), P("exp", None), weights, weights),
        check_vma=False,
    )
```

```python
import functools

import jax
import jax.numpy as jnp
from jax import lax
from jax.experimental import pallas as pl
from jax.experimental.pallas import tpu as pltpu
from jax.sharding import PartitionSpec as P

MESH = pl.DeviceIdType.MESH
F32 = jnp.float32
BF16 = jnp.bfloat16


def loop(count, step, first=0):
    def run(i, carry):
        step(i)
        return carry

    lax.fori_loop(first, first + count, run, 0)


SIDE = 4
SHIFTS = (
    (2, 2), (1, 2), (3, 2), (2, 0), (0, 2), (1, 0), (3, 0), (0, 0),
    (2, 1), (2, 3), (1, 1), (3, 3), (1, 3), (3, 1), (0, 1), (0, 3),
)
LINE = (1, 3, 2, 0)
PARTS = 3


def pick(i, values):
    found = jnp.int32(0)
    for n, value in enumerate(values):
        found = jnp.where(i == n, value, found)
    return found


def shift(i):
    return pick(i, [dy for dy, _ in SHIFTS]), pick(i, [dx for _, dx in SHIFTS])


def layer_kernel(
    nt, ne, rows_dev, hid, cols, htile, ntile,
    sw, xt, gt, p2,
    relay1, relay2, wout, trecv, gpart, gstage,
    xg, ww, pa, pat, dw, cbuf, ring1, ring2, spare, wt, pr, grow,
    s1, r1, sx, tr, sup, sdn, sf, gs, gq, gx, s2, wr, ps, prs, s3, r2, sg, gr, cs, cr, qs, qr, ts, trr, fs, fr,
):
    t = lax.axis_index("tok")
    e = lax.axis_index("exp")
    z, k = lax.div(e, 2), lax.rem(e, 2)
    y, x = lax.div(t, SIDE), lax.rem(t, SIDE)
    q, h = lax.div(t, 2), lax.rem(t, 2)
    nz, ny = ne // 2, nt // SIDE
    sibling = 2 * z + 1 - k
    column_core = 2 * z + h
    above = lax.rem(y + 1, ny) * SIDE + x
    below = lax.rem(y + ny - 1, ny) * SIDE + x

    def remote(src, dst, send, recv, tok, ex):
        return pltpu.make_async_remote_copy(
            src_ref=src, dst_ref=dst, send_sem=send, recv_sem=recv,
            device_id=(tok, ex), device_id_type=MESH,
        )

    def push(src, dst, send, recv, tok, ex):
        own = jnp.logical_and(tok == t, ex == e)

        @pl.when(own)
        def _():
            pltpu.make_async_copy(src, dst, recv).start()

        @pl.when(jnp.logical_not(own))
        def _():
            remote(src, dst, send, recv, tok, ex).start()

    def sent(src, dst, send, recv, tok, ex):
        @pl.when(jnp.logical_not(jnp.logical_and(tok == t, ex == e)))
        def _():
            remote(src, dst, send, recv, tok, ex).wait_send()

    def landed(dst, recv):
        pltpu.make_async_copy(dst, dst, recv).wait()

    def place_of(tok):
        return lax.rem(tok, 2) * ne + lax.div(tok, 2)

    def rows(block):
        return pl.ds(pl.multiple_of(place_of(block) * rows_dev, rows_dev), rows_dev)

    def pair_rows(row, core):
        return pl.ds(pl.multiple_of((core * ne + 2 * row) * rows_dev, 2 * rows_dev), 2 * rows_dev)

    def target(i):
        dy, dx = shift(i)
        return lax.rem(y + dy, ny) * SIDE + lax.rem(x + dx, SIDE)

    def origin(i):
        dy, dx = shift(i)
        return lax.rem(y + ny - dy, ny) * SIDE + lax.rem(x + SIDE - dx, SIDE)

    barrier = pltpu.get_barrier_semaphore()

    def greet_plane(i):
        tok, ex = lax.div(i, 2), 2 * z + lax.rem(i, 2)

        @pl.when(jnp.logical_not(jnp.logical_and(tok == t, ex == e)))
        def _():
            pl.semaphore_signal(barrier, inc=1, device_id=(tok, ex), device_id_type=MESH)

    def greet_line(ex):
        @pl.when(lax.div(ex, 2) != z)
        def _():
            pl.semaphore_signal(barrier, inc=1, device_id=(t, ex), device_id_type=MESH)

    loop(2 * nt, greet_plane)
    loop(ne, greet_line)
    pl.semaphore_wait(barrier, 2 * nt - 1 + ne - 2)

    def token_part(a, block):
        return xg.at[a, rows(block), :]

    def row_copy(i):
        return (xt, token_part(0, t), sx.at[i], tr.at[2 * t], y * SIDE + k + 2 * i, column_core)

    def ring_copy(block, sem, tok):
        part = token_part(0, block)
        return remote(part, part, sem, tr.at[2 * block], tok, e)

    def row_at(dy):
        return lax.rem(y + dy, ny)

    def swing_copy(n):
        return remote(gt, gstage.at[y], gs.at[n], gq.at[n], (above, below)[n], e)

    def pass_copy(n):
        part = gstage.at[row_at((ny - 1, 1)[n]), pl.ds(n * (rows_dev // 2), rows_dev // 2), :]
        return remote(part, part, gs.at[2 + n], gq.at[2 + n], (above, below)[n], e)

    def side_copy(dy, i):
        row = row_at(dy)
        block = row * SIDE + x
        src = gt if dy == 0 else gstage.at[row]
        return (src, token_part(1, block), gx.at[2 * dy + i], tr.at[2 * block + 1], y * SIDE + k + 2 * i, column_core)

    def side(dy):
        for i in range(2):
            push(*side_copy(dy, i))

    def twin_copy(a, block, i):
        part = token_part(a, block)
        return remote(part, part, sf.at[2 * i + a], tr.at[2 * block + a], t, sibling)

    def row_block(dy, w):
        return lax.rem(y + dy, ny) * SIDE + k + 2 * w

    def line_copy(s, i):
        hs, j = lax.div(i, ne), lax.rem(i, ne)
        half, core = lax.rem(x + hs, 2), lax.rem(j, 2)
        plane = lax.rem(z + pick(lax.div(j, 2), LINE), nz)
        piece = (2 * plane + half) * 2 + core
        m = half * ne + e
        return (
            sw.at[piece, s], relay1.at[m, s], s1.at[2 * ne * s + i], r1.at[2 * ne * s + m], t, 2 * plane + core,
        )

    def plane_copy(s, i):
        tok = target(i)
        return (
            relay1.at[place_of(tok), s], ww.at[s, :, rows(t), :], s2.at[nt * s + i], wr.at[nt * s + t], tok, e,
        )

    prob_copy = remote(p2.at[1 - k], pr, ps, prs, t, sibling)
    prob_copy.start()
    for n in range(2):
        swing_copy(n).start()
    loop(2, lambda i: push(*row_copy(i)))
    side(0)

    def send_line(s):
        loop(2 * ne, lambda i: push(*line_copy(s, i)))

    send_line(0)
    send_line(1)

    def forward_row(i):
        block = row_block(0, i)
        landed(token_part(0, block), tr.at[2 * block])
        twin_copy(0, block, i).start()
        ring_copy(block, sup.at[i], above).start()
        ring_copy(block, sdn.at[i], below).start()

    def forward_ring():
        lower, upper = row_block(ny - 1, 0), row_block(1, 1)
        landed(token_part(0, lower), tr.at[2 * lower])
        ring_copy(lower, sup.at[2], above).start()
        twin_copy(0, lower, 2).start()
        landed(token_part(0, upper), tr.at[2 * upper])
        ring_copy(upper, sdn.at[2], below).start()
        twin_copy(0, upper, 3).start()

    def forward_swing():
        for n, dy in enumerate((ny - 1, 1)):
            landed(gstage.at[row_at(dy)], gq.at[n])
            pass_copy(n).start()
            side(dy)

    def forward_pass():
        for n in range(2):
            part = gstage.at[row_at(2), pl.ds(n * (rows_dev // 2), rows_dev // 2), :]
            landed(part, gq.at[2 + n])
        side(2)

    def twin_row(dy):
        def step(w):
            block = row_block(dy, w)
            landed(token_part(1, block), tr.at[2 * block + 1])
            twin_copy(1, block, 2 * dy + w).start()

        loop(2, step)

    def forward_weights(s):
        def step(i):
            m = place_of(target(i))
            landed(relay1.at[m, s], r1.at[2 * ne * s + m])
            push(*plane_copy(s, i))

        loop(nt, step)

    forward_swing()
    loop(2, forward_row)
    forward_weights(0)
    forward_pass()
    send_line(2)
    twin_row(0)
    forward_ring()
    forward_weights(1)
    for dy in range(1, ny):
        twin_row(dy)
    late = ((ny - 1, 1), (1, 0), (2, 0), (2, 1))
    for n, (dy, w) in enumerate(late):
        block = row_block(dy, w)
        landed(token_part(0, block), tr.at[2 * block])
        twin_copy(0, block, 4 + n).start()
    forward_weights(2)

    def take_tokens(i):
        block = 2 * i + 1 - k
        for a in range(2):
            landed(token_part(a, block), tr.at[2 * block + a])

    loop(nt // 2, take_tokens)
    prob_copy.wait()

    grow[...] = jnp.zeros_like(grow)
    mine = jnp.where(k == h, 1.0, 0.0).astype(F32)

    def hidden(s):
        units = pl.ds(s * htile, htile)
        loop(nt, lambda i: landed(ww.at[s, :, rows(i), :], wr.at[nt * s + i]))
        wt[0] = ww[s, 0].T
        wt[1] = ww[s, 1].T

        def strip(ni):
            lanes = pl.ds(pl.multiple_of(ni * ntile, ntile), ntile)
            pre = jnp.dot(wt[0], xg[0, :, lanes], preferred_element_type=F32)
            hg = jnp.dot(wt[1], xg[1, :, lanes], preferred_element_type=F32)
            prob = p2[k, :, lanes] * mine + pr[:, lanes] * (1.0 - mine)
            sig = 1.0 / (1.0 + jnp.exp(-pre))
            act = (pre * sig).astype(BF16).astype(F32)
            slope = sig * (1.0 + pre * (1.0 - sig))
            grad = (prob * hg * slope).astype(BF16)
            pa[units, lanes] = grad
            pat[0, lanes, :] = grad.T
            pat[1, lanes, :] = (prob * act).astype(BF16).T
            grow[:, lanes] = grow[:, lanes] + jnp.sum(act * hg, axis=0, keepdims=True)

        loop(cols // ntile, strip)

    def gate_copy(i):
        j = 2 * q + k
        return (grow, gpart.at[j], sg.at[i], gr.at[j], target(i), column_core)

    def grad_copy(s, i):
        block = target(i)
        m = h * ne + q
        return (dw.at[s, :, rows(block), :], relay2.at[m, s], s3.at[nt * s + i], r2.at[2 * ne * s + m], block, e)

    def weight_grads(s):
        def step(i):
            part = rows(target(i))
            for a in range(2):
                dw[s, a, part, :] = jnp.dot(xg[a, part, :], pat[a], preferred_element_type=F32).astype(BF16)
            push(*grad_copy(s, i))

        loop(nt, step)

    def owner_copy(s, i):
        tok = origin(i)
        piece = (2 * z + lax.rem(tok, 2)) * 2 + k
        return (
            relay2.at[place_of(tok), s], wout.at[piece, s], fs.at[nt * s + i], fr.at[2 * ne * s + piece],
            t, lax.div(tok, 2),
        )

    def forward_grads(s, count=nt, first=0):
        def step(i):
            m = place_of(origin(i))
            landed(relay2.at[m, s], r2.at[2 * ne * s + m])
            push(*owner_copy(s, i))

        loop(count, step, first)

    def token_part_grads(part):
        weights = jnp.concatenate([ww[s, 0, part, :] for s in range(PARTS)], axis=1)
        return jnp.dot(weights, pa[...], preferred_element_type=F32)

    def pair_copy(n, dy):
        row = row_at(dy)
        src = spare.at[0] if n == 0 else xg.at[0, pair_rows(row, 1 - k), :]
        return remote(src, cbuf.at[row], cs.at[n], cr.at[row], t, sibling)

    def give(n, dy):
        part = pair_rows(row_at(dy), 1 - k)
        if n == 0:
            spare[0] = token_part_grads(part).astype(BF16)
        else:
            xg[0, part, :] = token_part_grads(part).astype(BF16)
        pair_copy(n, dy).start()

    def half_rows(row, w):
        return rows(row * SIDE + k + 2 * w)

    def keep(dy, added):
        row = row_at(dy)
        landed(cbuf.at[row], cr.at[row])
        for w in range(2):
            part = half_rows(row, w)
            total = token_part_grads(part)
            total = total + cbuf[row, w * rows_dev:(w + 1) * rows_dev, :].astype(F32)
            for term in added[w]:
                total = total + term[...].astype(F32)
            if dy == 2:
                spare[1, w * rows_dev:(w + 1) * rows_dev, :] = total.astype(BF16)
            else:
                xg[0, part, :] = total.astype(BF16)

    def far_copy(w):
        src = spare.at[1, pl.ds(w * rows_dev, rows_dev), :]
        return remote(src, ring1.at[1 - w], qs.at[w], qr.at[1 - w], (below, above)[w], e)

    def near_copy(n):
        src = xg.at[0, pair_rows(row_at((1, ny - 1)[n]), k), :]
        return remote(src, ring2.at[n], qs.at[2 + n], qr.at[2 + n], (above, below)[n], e)

    def row_owner(w):
        return (
            xg.at[0, half_rows(y, w), :], trecv.at[lax.div(x, 2)], ts.at[w], trr.at[lax.div(x, 2)],
            y * SIDE + k + 2 * w, column_core,
        )

    gives = (2, 1, ny - 1, 0)
    quarter = nt // 4
    last = PARTS - 1
    for s in range(last):
        hidden(s)
        weight_grads(s)
    hidden(last)
    give(0, 2)
    keep(2, ((), ()))
    for w in range(2):
        far_copy(w).start()
    weight_grads(last)
    forward_grads(0)
    loop(nt, lambda i: push(*gate_copy(i)))
    for i in range(3):
        ring_copy(t, sup.at[i], above).wait_send()
        ring_copy(t, sdn.at[i], below).wait_send()
    for a in range(2):
        loop(nt // 2, lambda i: twin_copy(a, t, i).wait_send())
    for n, dy in enumerate(gives):
        if n > 0:
            give(n, dy)
    forward_grads(last - 1)
    landed(ring1.at[0], qr.at[0])
    keep(1, ((), (ring1.at[0],)))
    near_copy(0).start()
    forward_grads(last, quarter)
    landed(ring1.at[1], qr.at[1])
    keep(ny - 1, ((ring1.at[1],), ()))
    near_copy(1).start()
    forward_grads(last, 2 * quarter, quarter)
    for n in range(2):
        landed(ring2.at[n], qr.at[2 + n])
    both = [[ring2.at[n, pl.ds(w * rows_dev, rows_dev), :] for n in range(2)] for w in range(2)]
    keep(0, both)
    for w in range(2):
        push(*row_owner(w))
    forward_grads(last, quarter, 3 * quarter)

    for s in range(PARTS):
        loop(2 * ne, lambda i: landed(wout.at[i, s], fr.at[2 * ne * s + i]))
    loop(2, lambda i: landed(trecv.at[i], trr.at[i]))
    loop(nt, lambda i: landed(gpart.at[i], gr.at[i]))
    loop(nt, lambda i: sent(*gate_copy(i)))
    loop(2, lambda i: sent(*row_copy(i)))
    for n in range(2):
        swing_copy(n).wait_send()
        pass_copy(n).wait_send()
    for dy in range(ny):
        for i in range(2):
            sent(*side_copy(dy, i))
    for s in range(PARTS):
        loop(2 * ne, lambda i: sent(*line_copy(s, i)))
        loop(nt, lambda i: sent(*plane_copy(s, i)))
        loop(nt, lambda i: sent(*grad_copy(s, i)))
        loop(nt, lambda i: sent(*owner_copy(s, i)))
    for n, dy in enumerate(gives):
        pair_copy(n, dy).wait_send()
    for n in range(2):
        far_copy(n).wait_send()
        near_copy(n).wait_send()
    for w in range(2):
        sent(*row_owner(w))


def layer(sw, xt, gt, p2, nt, ne):
    _, _, _, rows_dev, htile = sw.shape
    hid = PARTS * htile
    cols = xt.shape[1]
    width = nt * rows_dev
    ny = nt // SIDE
    ntile = min(512, cols)
    dma = pltpu.SemaphoreType.DMA
    anywhere = pl.BlockSpec(memory_space=pl.ANY)
    relay = jax.ShapeDtypeStruct(sw.shape, BF16)
    counts = (6 * ne, 6 * ne, 2, 2 * nt, 3, 3, nt, 4, 4, 2 * ny, 3 * nt, 3 * nt)
    counts_back = (3 * nt, 6 * ne, nt, nt, ny, ny, 4, 4, 2, 2, 3 * nt, 6 * ne)
    return pl.pallas_call(
        functools.partial(layer_kernel, nt, ne, rows_dev, hid, cols, htile, ntile),
        out_shape=(
            relay,
            relay,
            relay,
            jax.ShapeDtypeStruct((2, rows_dev, cols), BF16),
            jax.ShapeDtypeStruct((nt, 1, cols), F32),
            jax.ShapeDtypeStruct((ny, rows_dev, cols), BF16),
        ),
        in_specs=[anywhere] * 3 + [pl.BlockSpec(memory_space=pltpu.VMEM)],
        out_specs=(anywhere,) * 6,
        scratch_shapes=[
            pltpu.VMEM((2, width, cols), BF16),
            pltpu.VMEM((PARTS, 2, width, htile), BF16),
            pltpu.VMEM((hid, cols), BF16),
            pltpu.VMEM((2, cols, htile), BF16),
            pltpu.VMEM((PARTS, 2, width, htile), BF16),
            pltpu.VMEM((ny, 2 * rows_dev, cols), BF16),
            pltpu.VMEM((2, rows_dev, cols), BF16),
            pltpu.VMEM((2, 2 * rows_dev, cols), BF16),
            pltpu.VMEM((2, 2 * rows_dev, cols), BF16),
            pltpu.VMEM((2, htile, width), BF16),
            pltpu.VMEM((1, cols), F32),
            pltpu.VMEM((1, cols), F32),
            *[dma((count,)) for count in counts],
            dma,
            dma,
            *[dma((count,)) for count in counts_back],
        ],
        compiler_params=pltpu.CompilerParams(
            collective_id=0, has_side_effects=True, vmem_limit_bytes=60 * 1024 * 1024
        ),
        cost_estimate=pl.CostEstimate(
            flops=10 * width * hid * cols, bytes_accessed=64 << 20, transcendentals=hid * cols
        ),
    )(sw, xt, gt, p2)


def take_kernel(ids, up, down, out):
    htile = out.shape[-1]
    for s in range(PARTS):
        for a, weight in enumerate((up, down)):
            out[0, s, a] = weight[0, :, s * htile:(s + 1) * htile]


def take(ids, up_weight, down_weight):
    _, rows_dev, hid = up_weight.shape
    count = ids.shape[0]
    block = (1, PARTS, 2, rows_dev, hid // PARTS)
    return pl.pallas_call(
        take_kernel,
        out_shape=jax.ShapeDtypeStruct((count, *block[1:]), BF16),
        grid_spec=pltpu.PrefetchScalarGridSpec(
            num_scalar_prefetch=1,
            grid=(count,),
            in_specs=[pl.BlockSpec((1, rows_dev, hid), lambda i, ids: (ids[i], 0, 0))] * 2,
            out_specs=pl.BlockSpec(block, lambda i, ids: (i, 0, 0, 0, 0)),
        ),
    )(ids, up_weight, down_weight)


def combine_kernel(ids, pieces, up_out, down_out, total):
    htile = pieces.shape[-1]
    total[...] = jnp.zeros_like(total)
    for n in range(pieces.shape[0]):
        expert = ids[n]
        for s in range(PARTS):
            units = slice(s * htile, (s + 1) * htile)
            for a in range(2):
                total[a, expert, :, units] = total[a, expert, :, units] + pieces[n, s, a].astype(F32)
    up_out[...] = total[0].astype(BF16)
    down_out[...] = total[1].astype(BF16)


def combine(ids, pieces, experts):
    count, parts, _, rows_dev, htile = pieces.shape
    hid = parts * htile
    tile = 32 if rows_dev % 32 == 0 else 16
    out = jax.ShapeDtypeStruct((experts, rows_dev, hid), BF16)
    return pl.pallas_call(
        combine_kernel,
        out_shape=(out, out),
        grid_spec=pltpu.PrefetchScalarGridSpec(
            num_scalar_prefetch=1,
            grid=(rows_dev // tile,),
            in_specs=[pl.BlockSpec((count, parts, 2, tile, htile), lambda i, ids: (0, 0, 0, i, 0))],
            out_specs=[pl.BlockSpec((experts, tile, hid), lambda i, ids: (0, i, 0))] * 2,
            scratch_shapes=[pltpu.VMEM((2, experts, tile, hid), F32)],
        ),
        compiler_params=pltpu.CompilerParams(vmem_limit_bytes=32 * 1024 * 1024),
    )(ids, pieces)


def body(tokens, grad_out, gate_probs, routes, need_lists, up_weight, down_weight):
    nt, ne = lax.axis_size("tok"), lax.axis_size("exp")
    t, e = lax.axis_index("tok"), lax.axis_index("exp")
    experts = up_weight.shape[0]
    need = need_lists.reshape(ne, ne, nt // ne)
    ids = (jnp.take(need, e, axis=1) - e * experts).reshape(-1)
    sw = take(ids, up_weight, down_weight)
    slots = 2 * (t // 2) + jnp.arange(2, dtype=jnp.int32)
    p2 = jnp.sum(jnp.where(routes[None] == slots[:, None, None], gate_probs[None], 0.0), axis=2)
    _, _, wout, trecv, gpart, _ = layer(sw, tokens.T, grad_out.T, p2[:, None, :], nt, ne)
    token_grads = jnp.sum(trecv.astype(F32), axis=0).astype(BF16).T
    slot_ids = jnp.arange(nt, dtype=jnp.int32)
    hits = routes[None] == slot_ids[:, None, None]
    gate_grads = jnp.sum(jnp.where(hits, gpart.reshape(nt, -1, 1), 0.0), axis=0)
    up_grads, down_grads = combine(ids, wout, experts)
    return (token_grads, gate_grads, up_grads, down_grads)


def solution(mesh):
    split = (P("exp", "tok"), P("exp", "tok"), P("exp", None), P("exp", None))
    weights = P("exp", "tok", None)
    return jax.shard_map(
        body,
        mesh=mesh,
        in_specs=(*split, P(), weights, weights),
        out_specs=(P("exp", "tok"), P("exp", None), weights, weights),
        check_vma=False,
    )
```
